768 devices in a mesh: row: 32 (over z_lo, x, core), col: 24 (over y, z_hi).
Axes of the slice: x: 4, y: 8, z: 12 (z_hi: 3, z_lo: 4; z = z_hi * 4 + z_lo), core: 2. Of those that a mesh axis runs over, the one named last changes fastest.
Arguments:
- populations: float32 [19, 512, 192, 128], P(None, 'row', 'col'), may hold values from 0.02 to 0.08
- link_mask: int32 [2, 512, 192, 128], P(None, 'row', 'col'), may hold values from 0 to 511, as said below
- sphere_of_cell: int32 [512, 192, 128], P('row', 'col'), may hold values from 0 to 2047, as said below
- sphere_velocity: float32 [24, 3, 2048], P('col', None, 'row'), may hold values from -0.05 to 0.05
Outputs:
- out_pops: float32 [19, 512, 192, 128], P(None, 'row', 'col')
- sphere_force: float32 [24, 3, 2048], P('col', None, 'row')
The draws below stay inside these ranges and needn't reach their ends.
Inputs may be any that keep to these rules, and one draw needn't show every extreme that they name: `link_mask`: any pattern of bits; a blocked link needn't match any sphere geometry. `sphere_of_cell`: for a cell at x, the id s satisfies s // 64 = (x // 16 + d) mod (32) for some d in -1, 0, 1.
All inputs are finite; a program needn't handle non-finite values.
Results may differ from the reference program's by a relative error of at most 0.0001.
Values sent between devices are 32-bit elements; how exact they have to be, the bound alone decides.
No kernel may reach another device: no remote copies, remote signals or barrier semaphores. Data moves between devices by JAX's collectives and lax.ppermute only.
A program may use at most 64 MiB of HBM per device.

```python
import jax
import jax.numpy as jnp

CX = 16
CY = 8
NZ = 128
SPH_DEV = 64
STEPS = 2
NX = 512
NY = 192
SPH_ROW = 2048
COL_TILES = 24


def draw_link_mask(key, part):
    first_bits = jax.random.randint(jax.random.fold_in(key, 11), (2, NX, NY, NZ), 0, 512, dtype=jnp.int32)
    second_bits = jax.random.randint(jax.random.fold_in(key, 12), (2, NX, NY, NZ), 0, 512, dtype=jnp.int32)
    linked = jnp.bitwise_and(first_bits, second_bits)
    position = jnp.arange(NX * NY * NZ, dtype=jnp.int32).reshape(1, NX, NY, NZ)
    linked = jnp.where(position == 0, 511, linked)
    return jnp.where(position == 1, 0, linked)


def draw_sphere_of_cell(key, part):
    tile_count = NX // CX
    step_off = jax.random.randint(jax.random.fold_in(key, 21), (NX, NY, NZ), -1, 2, dtype=jnp.int32)
    member = jax.random.randint(jax.random.fold_in(key, 22), (NX, NY, NZ), 0, SPH_DEV, dtype=jnp.int32)
    slab_index = (jnp.arange(NX, dtype=jnp.int32) // CX).reshape(NX, 1, 1)
    owner_tile = jnp.mod(slab_index + step_off, tile_count)
    result = owner_tile * SPH_DEV + member
    position = jnp.arange(NX * NY * NZ, dtype=jnp.int32).reshape(NX, NY, NZ)
    result = jnp.where(position == 0, 0, result)
    return jnp.where(position == (NX - 1) * NY * NZ, tile_count * SPH_DEV - 1, result)


def block_scale(key, dims, cuts, least, top_value):
    def one(dim, shards_of):
        steps = jax.random.uniform(jax.random.fold_in(jax.random.fold_in(key, 6), dim), (shards_of,), jnp.float32, least / len(cuts), top_value / len(cuts))
        return jnp.repeat(jnp.exp(steps), dims[dim] // shards_of).reshape((-1,) + (1,) * (len(dims) - dim - 1))

    level = one(*cuts[0])
    for cut in cuts[1:]:
        level = level * one(*cut)
    return level


def setup_inputs(seed: int = 0) -> dict:
    splits = jax.random.split(jax.random.key(seed), 5)
    populations = jnp.clip(0.02 + 0.06 * jax.random.uniform(splits[0], (19, NX, NY, NZ), jnp.float32) ** block_scale(splits[0], (19, NX, NY, NZ), ((1, 32), (2, 24)), -0.2, 0.2), 0.02, 0.08)
    link_mask = draw_link_mask(jax.random.fold_in(splits[4], 71), 0)
    sphere_of_cell = draw_sphere_of_cell(jax.random.fold_in(splits[4], 71), 0)
    sphere_velocity = jnp.clip(jax.random.uniform(splits[3], (COL_TILES, 3, SPH_ROW), jnp.float32, -0.05, 0.05) * block_scale(splits[3], (COL_TILES, 3, SPH_ROW), ((0, 24), (2, 32)), -0.4, 0.0), -0.05, 0.05)
    return dict(populations=populations, link_mask=link_mask, sphere_of_cell=sphere_of_cell, sphere_velocity=sphere_velocity)


lattice_dirs = ((0, 0, 0), (1, 0, 0), (-1, 0, 0), (0, 1, 0), (0, -1, 0), (0, 0, 1), (0, 0, -1),
                (1, 1, 0), (-1, -1, 0), (1, -1, 0), (-1, 1, 0), (1, 0, 1), (-1, 0, -1),
                (1, 0, -1), (-1, 0, 1), (0, 1, 1), (0, -1, -1), (0, 1, -1), (0, -1, 1))
lattice_weights = (1.0 / 3.0,) + (1.0 / 18.0,) * 6 + (1.0 / 36.0,) * 12
relax_rate = 1.25


def reverse_of(index):
    if index == 0:
        return 0
    return index + 1 if index % 2 == 1 else index - 1


def link_bit(link_mask, index):
    plane = (index - 1) // 9
    offset = (index - 1) % 9
    return jnp.bitwise_and(jnp.right_shift(link_mask[plane], offset), 1)


def project(direction, vectors):
    total = None
    for axis_n in range(3):
        if direction[axis_n] != 0:
            term = direction[axis_n] * vectors[axis_n]
            total = term if total is None else total + term
    return total


def collide(current):
    density = current[0]
    for index in range(1, 19):
        density = density + current[index]
    moment = []
    for axis_n in range(3):
        total = jnp.zeros_like(density)
        for index in range(19):
            if lattice_dirs[index][axis_n] != 0:
                total = total + lattice_dirs[index][axis_n] * current[index]
        moment.append(total / density)
    speed_sq = moment[0] * moment[0] + moment[1] * moment[1] + moment[2] * moment[2]
    relaxed = []
    for index in range(19):
        if index == 0:
            along = jnp.zeros_like(density)
        else:
            along = project(lattice_dirs[index], moment)
        equil = lattice_weights[index] * density * (1.0 + 3.0 * along + 4.5 * along * along - 1.5 * speed_sq)
        relaxed.append(current[index] - relax_rate * (current[index] - equil))
    return relaxed


def reference(populations, link_mask, sphere_of_cell, sphere_velocity):
    height = populations.shape[3]
    z_coord = jnp.arange(height, dtype=jnp.int32).reshape(1, 1, height)
    y_tile = (jnp.arange(populations.shape[2], dtype=jnp.int32) // CY).reshape(1, -1, 1)
    cell_u = [sphere_velocity[y_tile, axis_n, sphere_of_cell] for axis_n in range(3)]
    current = [populations[index] for index in range(19)]
    link_force = [jnp.zeros(sphere_of_cell.shape, jnp.float32) for axis_n in range(3)]
    for repeat in range(STEPS):
        relaxed = collide(current)
        arrived = []
        for index in range(19):
            step_x, step_y, step_z = lattice_dirs[index]
            back = reverse_of(index)
            moved = jnp.roll(relaxed[index], (step_x, step_y, step_z), axis=(0, 1, 2))
            if step_z != 0:
                source_z = z_coord - step_z
                moved = jnp.where((source_z < 0) | (source_z >= height), relaxed[back], moved)
            if index > 0:
                along = project(lattice_dirs[index], cell_u)
                blocked = link_bit(link_mask, back) == 1
                moved = jnp.where(blocked, relaxed[back] + 6.0 * lattice_weights[index] * along, moved)
                hit = link_bit(link_mask, index).astype(jnp.float32)
                transfer = hit * (2.0 * relaxed[index] - 6.0 * lattice_weights[index] * along)
                for axis_n in range(3):
                    if lattice_dirs[index][axis_n] != 0:
                        link_force[axis_n] = link_force[axis_n] + lattice_dirs[index][axis_n] * transfer
            arrived.append(moved)
        current = arrived
    segment = (y_tile * SPH_ROW + sphere_of_cell).astype(jnp.int32).ravel()
    totals = []
    for axis_n in range(3):
        summed = jax.ops.segment_sum(link_force[axis_n].ravel(), segment, num_segments=COL_TILES * SPH_ROW)
        totals.append(summed.reshape(COL_TILES, SPH_ROW))
    return jnp.stack(current), jnp.stack(totals, axis=1)
```

```python
import functools

import jax
import jax.numpy as jnp
from jax import lax
from jax.experimental import pallas as pl
from jax.experimental.pallas import tpu as pltpu
from jax.sharding import PartitionSpec as P

DIRS = (
    (0, 0, 0),
    (1, 0, 0),
    (-1, 0, 0),
    (0, 1, 0),
    (0, -1, 0),
    (0, 0, 1),
    (0, 0, -1),
    (1, 1, 0),
    (-1, -1, 0),
    (1, -1, 0),
    (-1, 1, 0),
    (1, 0, 1),
    (-1, 0, -1),
    (1, 0, -1),
    (-1, 0, 1),
    (0, 1, 1),
    (0, -1, -1),
    (0, 1, -1),
    (0, -1, 1),
)
WEIGHTS = (1.0 / 3.0,) + (1.0 / 18.0,) * 6 + (1.0 / 36.0,) * 12
RELAX = 1.25
F32 = jnp.float32
CX, CY, NZ, PER = 16, 8, 128, 64
ROWS = CX * CY
XP = tuple(i for i in range(19) if DIRS[i][0] == 1)
XM = tuple(i for i in range(19) if DIRS[i][0] == -1)
YP = tuple(i for i in range(19) if DIRS[i][1] == 1)
YM = tuple(i for i in range(19) if DIRS[i][1] == -1)
YMSG = 264
VMEM_LIMIT = 40 * 1024 * 1024


def opp(i):
    return 0 if i == 0 else (i + 1 if i % 2 == 1 else i - 1)


def project(direction, vec):
    total = None
    for k in range(3):
        if direction[k] != 0:
            term = vec[k] if direction[k] == 1 else -vec[k]
            total = term if total is None else total + term
    return total


def bit_set(masks, j):
    return jnp.bitwise_and(masks[(j - 1) // 9], 1 << ((j - 1) % 9)) != 0


def wall_terms(vel):
    terms = [None] * 19
    for i in range(1, 19, 2):
        along = (6.0 * WEIGHTS[i]) * project(DIRS[i], vel)
        terms[i] = along
        terms[i + 1] = -along
    return terms


def moments(f):
    rho = f[0]
    for i in range(1, 19):
        rho = rho + f[i]
    mom = []
    for k in range(3):
        total = None
        for i in range(19):
            if DIRS[i][k] != 0:
                if total is None:
                    total = f[i]
                elif DIRS[i][k] == 1:
                    total = total + f[i]
                else:
                    total = total - f[i]
        mom.append(total)
    return rho, mom


def relaxed(f, which, rho, mom):
    inv = 1.0 / rho
    u = [m * inv for m in mom]
    base = 1.0 - 1.5 * (u[0] * u[0] + u[1] * u[1] + u[2] * u[2])
    out = {}
    scaled = {w: (RELAX * w) * rho for w in sorted({WEIGHTS[i] for i in which})}
    for i in which:
        if i == 0:
            shape = base
        else:
            along = project(DIRS[i], u)
            shape = base + along * (3.0 + 4.5 * along)
        out[i] = (1.0 - RELAX) * f[i] + scaled[WEIGHTS[i]] * shape
    return out


def iota(shape, dim):
    return lax.broadcasted_iota(jnp.int32, shape, dim)


def roll(x, by, axis):
    return pltpu.roll(x, by % x.shape[axis], axis)


def slots(ids):
    count = lax.axis_size("row")
    block = jnp.right_shift(ids, 6) - lax.axis_index("row") + 1
    block = jnp.where(block < 0, block + count, block)
    block = jnp.where(block >= count, block - count, block)
    return block, jnp.bitwise_and(ids, PER - 1)


def tables(left, own, right, shape):
    low = iota((8, NZ), 1) < PER
    pair = jnp.where(low, left, roll(own, PER, 1))
    near = [jnp.broadcast_to(pair[k : k + 1], shape) for k in range(3)]
    far = [jnp.broadcast_to(right[k : k + 1], shape) for k in range(3)]
    return near, far


def velocity_of(ids, near, far):
    block, member = slots(ids)
    index = jnp.where(block == 1, member + PER, member)
    is_far = block == 2
    out = []
    for k in range(3):
        a = jnp.take_along_axis(near[k], index, axis=1, mode="promise_in_bounds")
        b = jnp.take_along_axis(far[k], index, axis=1, mode="promise_in_bounds")
        out.append(jnp.where(is_far, b, a))
    return out


def z_edge(shape, step):
    return iota(shape, 1) == (0 if step == 1 else NZ - 1)


def plane_at(ref, i, x):
    start = x * CY if isinstance(x, int) else pl.multiple_of(x * CY, CY)
    return ref[i, pl.ds(start, CY), :]


def put_plane(ref, i, x, value):
    start = x * CY if isinstance(x, int) else pl.multiple_of(x * CY, CY)
    ref[i, pl.ds(start, CY), :] = value


def x_row(ref, i, y):
    return ref[i, pl.ds(y, CX, stride=CY), :]


def x_shifted(row, step, left, right):
    if step == 0:
        return row
    at = iota((CX, NZ), 0)
    if step == 1:
        return jnp.where(at == 0, left, roll(row, 1, 0))
    return jnp.where(at == CX - 1, right, roll(row, -1, 0))


def face_kernel(first_ref, last_ref, vel_ref, up_ref, down_ref):
    for ref, out, which in ((last_ref, up_ref, XP), (first_ref, down_ref, XM)):
        f = [ref[i] for i in range(19)]
        fs = relaxed(f, which, *moments(f))
        for n, i in enumerate(which):
            out[n] = fs[i]
        out[5] = jnp.zeros((CY, NZ), F32)
        out[5, 0:3, 0:PER] = vel_ref[...]


def collide_kernel(pop_ref, fs_ref):
    def body(x, carry):
        f = [plane_at(pop_ref, i, x) for i in range(19)]
        fs = relaxed(f, range(19), *moments(f))
        for i in range(19):
            put_plane(fs_ref, i, x, fs[i])
        return carry

    lax.fori_loop(0, CX, body, 0)


def row_kernel(fs_ref, mask_ref, id_ref, left_ref, right_ref, own_ref, up_ref, down_ref):
    shape = (CX, NZ)
    near, far = tables(left_ref[5], own_ref[5], right_ref[5], shape)
    for y, outward, missing, inner, out in ((CY - 1, YP, YM, CY - 2, up_ref), (0, YM, YP, 1, down_ref)):
        fs = [x_row(fs_ref, i, y) for i in range(19)]
        masks = [x_row(mask_ref, p, y) for p in range(2)]
        wall = wall_terms(velocity_of(id_ref[pl.ds(y, CX, stride=CY), :], near, far))
        f = [fs[0]]
        for i in range(1, 19):
            cx, cy, cz = DIRS[i]
            back = fs[opp(i)]
            if i in missing:
                moved = jnp.zeros(shape, F32)
            else:
                src_y = inner if i in outward else y
                moved = x_row(fs_ref, i, src_y) if i in outward else fs[i]
                if cx == 1:
                    moved = x_shifted(moved, 1, left_ref[XP.index(i), src_y : src_y + 1, :], None)
                elif cx == -1:
                    moved = x_shifted(moved, -1, None, right_ref[XM.index(i), src_y : src_y + 1, :])
            if cz != 0:
                if i not in missing:
                    moved = roll(moved, cz, 1)
                moved = jnp.where(z_edge(shape, cz), back, moved)
            f.append(jnp.where(bit_set(masks, opp(i)), back + wall[i], moved))
        rho, mom = moments(f)
        for n, i in enumerate(outward):
            out[n * CX : (n + 1) * CX, :] = fs[i]
            out[(5 + n) * CX : (6 + n) * CX, :] = f[i]
        for n, total in enumerate((rho, *mom)):
            out[(10 + n) * CX : (11 + n) * CX, :] = total
        for p in range(2):
            out[(14 + p) * CX : (15 + p) * CX, :] = masks[p].astype(F32)
        out[256:264, :] = jnp.zeros((8, NZ), F32)
        for i in outward:
            if DIRS[i][0] == 1:
                out[256:257, :] = left_ref[XP.index(i), y : y + 1, :]
            elif DIRS[i][0] == -1:
                out[257:258, :] = right_ref[XM.index(i), y : y + 1, :]


def arrive(fs, source, halo_row, masks, wall):
    shape = (CY, NZ)
    sub = iota(shape, 0)
    f = [fs[0]]
    for i in range(1, 19):
        cx, cy, cz = DIRS[i]
        back = fs[opp(i)]
        moved = source(i)
        if cy != 0:
            moved = roll(moved, cy, 0)
            edge = sub == (0 if cy == 1 else CY - 1)
            moved = jnp.where(edge, halo_row(i), moved)
        if cz != 0:
            moved = jnp.where(z_edge(shape, cz), back, roll(moved, cz, 1))
        f.append(jnp.where(bit_set(masks, opp(i)), back + wall[i], moved))
    return f


def first_step_kernel(fs_ref, mask_ref, id_ref, left_ref, right_ref, own_ref, f_ref, vel_ref, force_ref):
    shape = (CY, NZ)
    near, far = tables(left_ref[5], own_ref[5], right_ref[5], shape)

    def plane(x, source):
        fs = [plane_at(fs_ref, i, x) for i in range(19)]
        masks = [plane_at(mask_ref, p, x) for p in range(2)]
        start = x * CY if isinstance(x, int) else pl.multiple_of(x * CY, CY)
        vel = velocity_of(id_ref[pl.ds(start, CY), :], near, far)
        wall = wall_terms(vel)
        f = arrive(fs, source, lambda i: 0.0, masks, wall)
        for i in range(19):
            put_plane(f_ref, i, x, f[i])
        force = [jnp.zeros(shape, F32) for k in range(3)]
        for i in range(1, 19):
            term = jnp.where(bit_set(masks, i), 2.0 * (fs[i] - wall[i]), 0.0)
            for k in range(3):
                if DIRS[i][k] == 1:
                    force[k] = force[k] + term
                elif DIRS[i][k] == -1:
                    force[k] = force[k] - term
        for k in range(3):
            put_plane(vel_ref, k, x, vel[k])
            put_plane(force_ref, k, x, force[k])

    def inner(x, carry):
        plane(x, lambda i: plane_at(fs_ref, i, x - DIRS[i][0]))
        return carry

    plane(0, lambda i: left_ref[XP.index(i)] if i in XP else plane_at(fs_ref, i, 0 - DIRS[i][0]))
    lax.fori_loop(1, CX - 1, inner, 0)
    plane(CX - 1, lambda i: right_ref[XM.index(i)] if i in XM else plane_at(fs_ref, i, CX - 1 - DIRS[i][0]))


HI, LO = 6, 32


def second_step_kernel(
    fs_ref, f_ref, mask_ref, id_ref, force_ref, left_ref, right_ref, below_ref, above_ref,
    fs2_ref, halo_ref, up_ref, down_ref, mine_ref, fix_ref, a_ref, b_ref,
):
    shape = (CX, NZ)
    for side, (y, inward, outward, got) in enumerate(((0, YP, YM, below_ref), (CY - 1, YM, YP, above_ref))):
        masks = [got[(14 + p) * CX : (15 + p) * CX, :].astype(jnp.int32) for p in range(2)]
        rho = got[10 * CX : 11 * CX, :]
        mom = [got[(11 + k) * CX : (12 + k) * CX, :] for k in range(3)]
        for i in outward:
            cx, cy, cz = DIRS[i]
            moved = x_row(fs_ref, i, y)
            if cx == 1:
                moved = x_shifted(moved, 1, left_ref[XP.index(i), y : y + 1, :], None)
            elif cx == -1:
                moved = x_shifted(moved, -1, None, right_ref[XM.index(i), y : y + 1, :])
            held = bit_set(masks, opp(i))
            if cz != 0:
                moved = roll(moved, cz, 1)
                held = jnp.logical_or(held, z_edge(shape, cz))
            moved = jnp.where(held, 0.0, moved)
            rho = rho + moved
            for k in range(3):
                if DIRS[i][k] == 1:
                    mom[k] = mom[k] + moved
                elif DIRS[i][k] == -1:
                    mom[k] = mom[k] - moved
        f = {i: got[(5 + n) * CX : (6 + n) * CX, :] for n, i in enumerate(inward)}
        beyond = relaxed(f, inward, rho, mom)
        masks = [x_row(mask_ref, p, y) for p in range(2)]
        for n, i in enumerate(inward):
            halo_ref[side * 5 + n] = beyond[i]
            cx, cy, cz = DIRS[i]
            moved = x_shifted(got[n * CX : (n + 1) * CX, :], cx, got[256:257, :], got[257:258, :])
            held = bit_set(masks, opp(i))
            if cz != 0:
                moved = roll(moved, cz, 1)
                held = jnp.logical_or(held, z_edge(shape, cz))
            fix_ref[side * 5 + n] = jnp.where(held, 0.0, moved)

    sub = iota((CY, NZ), 0)

    def body(x, carry):
        f = [plane_at(f_ref, i, x) for i in range(19)]
        for side, inward, at in ((0, YP, 0), (1, YM, CY - 1)):
            for n, i in enumerate(inward):
                f[i] = f[i] + jnp.where(sub == at, fix_ref[side * 5 + n, pl.ds(x, 1), :], 0.0)
        fs = relaxed(f, range(19), *moments(f))
        masks = [plane_at(mask_ref, p, x) for p in range(2)]
        hits = [None, None, None]
        for i in range(19):
            put_plane(fs2_ref, i, x, fs[i])
            if i > 0:
                term = jnp.where(bit_set(masks, i), fs[i], 0.0)
                for k in range(3):
                    if DIRS[i][k] == 0:
                        continue
                    if hits[k] is None:
                        hits[k] = term
                    elif DIRS[i][k] == 1:
                        hits[k] = hits[k] + term
                    else:
                        hits[k] = hits[k] - term
        start = pl.multiple_of(x * CY, CY)
        lanes = pl.ds(pl.multiple_of(x * NZ, NZ), NZ)
        block, member = slots(id_ref[pl.ds(start, CY), :])
        slot = block * PER + member
        hi, lo = jnp.right_shift(slot, 5), jnp.bitwise_and(slot, LO - 1)
        at_hi = [hi == h for h in range(HI)]
        for k in range(3):
            force = plane_at(force_ref, k, x) + 2.0 * hits[k]
            coarse = force.astype(jnp.bfloat16).astype(F32)
            for part, value in enumerate((coarse, force - coarse)):
                for h in range(0, HI, 2):
                    both = jnp.concatenate(
                        [jnp.where(at_hi[h], value, 0.0), jnp.where(at_hi[h + 1], value, 0.0)], axis=0
                    )
                    for h2 in range(2):
                        row = ((part * 2 + h2) * 9 + (h // 2) * 3 + k) * CY
                        a_ref[row : row + CY, lanes] = both[h2 * CY : (h2 + 1) * CY]
        for v in range(0, LO, 2):
            both = jnp.concatenate(
                [jnp.where(lo == v, 1.0, 0.0), jnp.where(lo == v + 1, 1.0, 0.0)], axis=0
            )
            b_ref[v * CY : (v + 2) * CY, lanes] = both.astype(jnp.bfloat16)
        return carry

    lax.fori_loop(0, CX, body, 0)

    cross = lax.dot_general(
        a_ref[...].astype(jnp.bfloat16), b_ref[...], (((1,), (1,)), ((), ())), preferred_element_type=F32
    )
    cross = cross[: 18 * CY] + cross[18 * CY :]
    same = jnp.bitwise_and(iota(cross.shape, 0), CY - 1) == jnp.bitwise_and(iota(cross.shape, 1), CY - 1)
    cross = jnp.where(same, cross, 0.0)
    column, lane = iota((LO * CY, NZ), 0), iota((LO * CY, NZ), 1)
    sums = None
    for h2 in range(2):
        pick = (jnp.right_shift(column, 3) + h2 * LO == lane).astype(F32)
        part = jnp.dot(
            cross[h2 * 9 * CY : (h2 + 1) * 9 * CY], pick, preferred_element_type=F32, precision=lax.Precision.HIGHEST
        )
        sums = part if sums is None else sums + part
    terms = [[jnp.sum(sums[(b * 3 + k) * CY : (b * 3 + k + 1) * CY], axis=0, keepdims=True) for k in range(3)] for b in range(3)]

    for out, which, x, block, corners in (
        (up_ref, XP, CX - 1, 2, (7, 9)),
        (down_ref, XM, 0, 0, (10, 8)),
    ):
        for n, i in enumerate(which):
            out[n] = plane_at(fs2_ref, i, x)
        rows = [
            halo_ref[YP.index(corners[0]), x : x + 1, :],
            halo_ref[5 + YM.index(corners[1]), x : x + 1, :],
            *terms[block],
        ]
        packed = jnp.zeros((CY, NZ), F32)
        for n, row in enumerate(rows):
            packed = jnp.where(sub == n, row, packed)
        out[5] = packed
    packed = jnp.zeros((CY, NZ), F32)
    for n, row in enumerate(terms[1]):
        packed = jnp.where(sub == n + 2, row, packed)
    mine_ref[...] = packed


def halo_slot(i):
    return YP.index(i) if DIRS[i][1] == 1 else 5 + YM.index(i)


def inner_planes_kernel(fs_ref, halo_ref, mask_ref, vel_ref, out_ref):
    def body(x, carry):
        fs = [plane_at(fs_ref, i, x) for i in range(19)]
        masks = [plane_at(mask_ref, p, x) for p in range(2)]
        wall = wall_terms([plane_at(vel_ref, k, x) for k in range(3)])
        f = arrive(
            fs,
            lambda i: plane_at(fs_ref, i, x - DIRS[i][0]),
            lambda i: halo_ref[halo_slot(i), pl.ds(x - DIRS[i][0], 1), :],
            masks,
            wall,
        )
        for i in range(19):
            put_plane(out_ref, i, x, f[i])
        return carry

    lax.fori_loop(1, CX - 1, body, 0)
    for x in (0, CX - 1):
        for i in range(19):
            put_plane(out_ref, i, x, plane_at(fs_ref, i, x))


def edge_planes_kernel(
    fs_ref, halo_ref, mask_ref, vel_ref, left_ref, right_ref, mine_ref, whole_ref, out_ref, force_ref
):
    del whole_ref

    def edge(local, x, far_ref, far_dirs):
        fs = [fs_ref[i, local * CY : (local + 1) * CY, :] for i in range(19)]
        masks = [mask_ref[p, local * CY : (local + 1) * CY, :] for p in range(2)]
        wall = wall_terms([vel_ref[k, local * CY : (local + 1) * CY, :] for k in range(3)])

        def source(i):
            if i in far_dirs:
                return far_ref[far_dirs.index(i)]
            at = local - DIRS[i][0]
            return fs_ref[i, at * CY : (at + 1) * CY, :]

        def halo_row(i):
            if i in far_dirs:
                n = 0 if DIRS[i][1] == 1 else 1
                return far_ref[5, n : n + 1, :]
            at = x - DIRS[i][0]
            return halo_ref[halo_slot(i), at : at + 1, :]

        f = arrive(fs, source, halo_row, masks, wall)
        for i in range(19):
            out_ref[i] = f[i]

    @pl.when(pl.program_id(0) == 0)
    def _():
        edge(0, 0, left_ref, XP)
        total = mine_ref[...] + left_ref[5] + right_ref[5]
        force_ref[...] = total[2:5, 0:PER]

    @pl.when(pl.program_id(0) == 1)
    def _():
        edge(1, CX - 1, right_ref, XM)


def params(**more):
    return pltpu.CompilerParams(vmem_limit_bytes=VMEM_LIMIT, **more)


def cost(flops, nbytes):
    return pl.CostEstimate(flops=flops, bytes_accessed=nbytes, transcendentals=0)


def shape(*dims):
    return jax.ShapeDtypeStruct(dims, F32)


def shift(x, axis, by):
    count = lax.axis_size(axis)
    return lax.ppermute(x, axis, [(i, (i + by) % count) for i in range(count)])


def on_device(populations, link_mask, sphere_of_cell, sphere_velocity):
    pops = populations.reshape(19, ROWS, NZ)
    mask = link_mask.reshape(2, ROWS, NZ)
    ids = sphere_of_cell.reshape(ROWS, NZ)
    vel = sphere_velocity.reshape(3, PER)
    cells = ROWS * NZ
    xmsg = (6, CY, NZ)

    to_right, to_left = pl.pallas_call(
        face_kernel,
        grid=(1,),
        in_specs=[
            pl.BlockSpec((19, CY, NZ), lambda g: (0, 0, 0)),
            pl.BlockSpec((19, CY, NZ), lambda g: (0, CX - 1, 0)),
            pl.BlockSpec((3, PER), lambda g: (0, 0)),
        ],
        out_specs=[pl.BlockSpec(xmsg, lambda g: (0, 0, 0))] * 2,
        out_shape=[shape(*xmsg)] * 2,
        compiler_params=params(),
        name="faces",
    )(pops, pops, vel)
    left = shift(to_right, "row", 1)
    right = shift(to_left, "row", -1)

    fs1 = pl.pallas_call(
        collide_kernel,
        out_shape=shape(19, ROWS, NZ),
        compiler_params=params(),
        cost_estimate=cost(300 * cells, 38 * 4 * cells),
        name="collide",
    )(pops)

    up, down = pl.pallas_call(
        row_kernel,
        out_shape=[shape(YMSG, NZ)] * 2,
        compiler_params=params(),
        name="y_rows",
    )(fs1, mask, ids, left, right, to_right)
    below = shift(up, "col", 1)
    above = shift(down, "col", -1)

    f1, cell_vel, force1 = pl.pallas_call(
        first_step_kernel,
        out_shape=[shape(19, ROWS, NZ), shape(3, ROWS, NZ), shape(3, ROWS, NZ)],
        compiler_params=params(),
        cost_estimate=cost(500 * cells, 50 * 4 * cells),
        name="first_step",
    )(fs1, mask, ids, left, right, to_right)

    fs2, halo, to_right2, to_left2, mine = pl.pallas_call(
        second_step_kernel,
        out_shape=[shape(19, ROWS, NZ), shape(10, CX, NZ), shape(*xmsg), shape(*xmsg), shape(CY, NZ)],
        scratch_shapes=[
            pltpu.VMEM((10, CX, NZ), F32),
            pltpu.VMEM((2 * 18 * CY, CX * NZ), F32),
            pltpu.VMEM((LO * CY, CX * NZ), jnp.bfloat16),
        ],
        compiler_params=params(),
        name="second_step",
    )(fs1, f1, mask, ids, force1, left, right, below, above)
    left2 = shift(to_right2, "row", 1)
    right2 = shift(to_left2, "row", -1)

    inner = pl.pallas_call(
        inner_planes_kernel,
        out_shape=shape(19, ROWS, NZ),
        compiler_params=params(),
        cost_estimate=cost(300 * cells, 45 * 4 * cells),
        name="inner_planes",
    )(fs2, halo, mask, cell_vel)

    last = CX // 2 - 1
    whole = pl.BlockSpec(xmsg, lambda g: (0, 0, 0))
    out, force = pl.pallas_call(
        edge_planes_kernel,
        grid=(2,),
        in_specs=[
            pl.BlockSpec((19, 2 * CY, NZ), lambda g: (0, g * last, 0)),
            pl.BlockSpec((10, CX, NZ), lambda g: (0, 0, 0)),
            pl.BlockSpec((2, 2 * CY, NZ), lambda g: (0, g * last, 0)),
            pl.BlockSpec((3, 2 * CY, NZ), lambda g: (0, g * last, 0)),
            whole,
            whole,
            pl.BlockSpec((CY, NZ), lambda g: (0, 0)),
            pl.BlockSpec(memory_space=pl.ANY),
        ],
        out_specs=[
            pl.BlockSpec((19, CY, NZ), lambda g: (0, g * (CX - 1), 0)),
            pl.BlockSpec((3, PER), lambda g: (0, 0)),
        ],
        out_shape=[shape(19, ROWS, NZ), shape(3, PER)],
        input_output_aliases={7: 0},
        compiler_params=params(),
        name="edge_planes",
    )(fs2, halo, mask, cell_vel, left2, right2, mine, inner)

    return out.reshape(19, CX, CY, NZ), force.reshape(1, 3, PER)


def solution(mesh):
    in_specs = (
        P(None, "row", "col", None),
        P(None, "row", "col", None),
        P("row", "col", None),
        P("col", None, "row"),
    )
    out_specs = (P(None, "row", "col", None), P("col", None, "row"))
    return jax.shard_map(on_device, mesh=mesh, in_specs=in_specs, out_specs=out_specs, check_vma=False)
```

```python
import jax
import jax.numpy as jnp
from jax import lax
from jax.experimental import pallas as pl
from jax.experimental.pallas import tpu as pltpu
from jax.sharding import PartitionSpec as P

DIRS = (
    (0, 0, 0),
    (1, 0, 0),
    (-1, 0, 0),
    (0, 1, 0),
    (0, -1, 0),
    (0, 0, 1),
    (0, 0, -1),
    (1, 1, 0),
    (-1, -1, 0),
    (1, -1, 0),
    (-1, 1, 0),
    (1, 0, 1),
    (-1, 0, -1),
    (1, 0, -1),
    (-1, 0, 1),
    (0, 1, 1),
    (0, -1, -1),
    (0, 1, -1),
    (0, -1, 1),
)
WEIGHTS = (1.0 / 3.0,) + (1.0 / 18.0,) * 6 + (1.0 / 36.0,) * 12
RELAX = 1.25
F32 = jnp.float32
CX, CY, NZ, PER = 16, 8, 128, 64
ROWS = CX * CY
XP = tuple(i for i in range(19) if DIRS[i][0] == 1)
XM = tuple(i for i in range(19) if DIRS[i][0] == -1)
YP = tuple(i for i in range(19) if DIRS[i][1] == 1)
YM = tuple(i for i in range(19) if DIRS[i][1] == -1)
YMSG = 264
VMEM_LIMIT = 40 * 1024 * 1024


def opp(i):
    return 0 if i == 0 else (i + 1 if i % 2 == 1 else i - 1)


def project(direction, vec):
    total = None
    for k in range(3):
        if direction[k] != 0:
            term = vec[k] if direction[k] == 1 else -vec[k]
            total = term if total is None else total + term
    return total


def bit_set(masks, j):
    return jnp.bitwise_and(masks[(j - 1) // 9], 1 << ((j - 1) % 9)) != 0


def wall_terms(vel):
    terms = [None] * 19
    for i in range(1, 19, 2):
        along = (6.0 * WEIGHTS[i]) * project(DIRS[i], vel)
        terms[i] = along
        terms[i + 1] = -along
    return terms


def moments(f):
    rho = f[0]
    for i in range(1, 19):
        rho = rho + f[i]
    mom = []
    for k in range(3):
        total = None
        for i in range(19):
            if DIRS[i][k] != 0:
                if total is None:
                    total = f[i]
                elif DIRS[i][k] == 1:
                    total = total + f[i]
                else:
                    total = total - f[i]
        mom.append(total)
    return rho, mom


def relaxed(f, which, rho, mom):
    inv = 1.0 / rho
    u = [m * inv for m in mom]
    base = 1.0 - 1.5 * (u[0] * u[0] + u[1] * u[1] + u[2] * u[2])
    out = {}
    scaled = {w: (RELAX * w) * rho for w in sorted({WEIGHTS[i] for i in which})}
    for i in which:
        if i == 0:
            shape = base
        else:
            along = project(DIRS[i], u)
            shape = base + along * (3.0 + 4.5 * along)
        out[i] = (1.0 - RELAX) * f[i] + scaled[WEIGHTS[i]] * shape
    return out


def iota(shape, dim):
    return lax.broadcasted_iota(jnp.int32, shape, dim)


def roll(x, by, axis):
    return pltpu.roll(x, by % x.shape[axis], axis)


def slots(ids):
    count = lax.axis_size("row")
    block = jnp.right_shift(ids, 6) - lax.axis_index("row") + 1
    block = jnp.where(block < 0, block + count, block)
    block = jnp.where(block >= count, block - count, block)
    return block, jnp.bitwise_and(ids, PER - 1)


def tables(left, own, right, shape):
    low = iota((8, NZ), 1) < PER
    pair = jnp.where(low, left, roll(own, PER, 1))
    near = [jnp.broadcast_to(pair[k : k + 1], shape) for k in range(3)]
    far = [jnp.broadcast_to(right[k : k + 1], shape) for k in range(3)]
    return near, far


def velocity_of(ids, near, far):
    block, member = slots(ids)
    index = jnp.where(block == 1, member + PER, member)
    is_far = block == 2
    out = []
    for k in range(3):
        a = jnp.take_along_axis(near[k], index, axis=1, mode="promise_in_bounds")
        b = jnp.take_along_axis(far[k], index, axis=1, mode="promise_in_bounds")
        out.append(jnp.where(is_far, b, a))
    return out


def z_edge(shape, step):
    return iota(shape, 1) == (0 if step == 1 else NZ - 1)


def plane_at(ref, i, x):
    start = x * CY if isinstance(x, int) else pl.multiple_of(x * CY, CY)
    return ref[i, pl.ds(start, CY), :]


def put_plane(ref, i, x, value):
    start = x * CY if isinstance(x, int) else pl.multiple_of(x * CY, CY)
    ref[i, pl.ds(start, CY), :] = value


def x_row(ref, i, y):
    return ref[i, pl.ds(y, CX, stride=CY), :]


def x_shifted(row, step, left, right):
    if step == 0:
        return row
    at = iota((CX, NZ), 0)
    if step == 1:
        return jnp.where(at == 0, left, roll(row, 1, 0))
    return jnp.where(at == CX - 1, right, roll(row, -1, 0))


def even_row():
    return lax.rem(lax.axis_index("row"), 2) == 0


class Either:
    def __init__(self, even, if_even, if_odd):
        self.even, self.if_even, self.if_odd = even, if_even, if_odd

    def __getitem__(self, at):
        return jnp.where(self.even, self.if_even[at], self.if_odd[at])


def neighbours(inner_ref, outer_ref):
    even = even_row()
    return Either(even, outer_ref, inner_ref), Either(even, inner_ref, outer_ref)


def put_messages(inner_ref, outer_ref, to_right, to_left):
    even = even_row()
    for n in range(6):
        inner_ref[n] = jnp.where(even, to_right[n], to_left[n])
        outer_ref[n] = jnp.where(even, to_left[n], to_right[n])


def face_kernel(pop_ref, vel_ref, inner_ref, outer_ref, face_ref, held_ref, sems):
    copies = [
        pltpu.make_async_copy(pop_ref.at[:, pl.ds(ROWS - CY, CY), :], face_ref.at[0], sems.at[0]),
        pltpu.make_async_copy(pop_ref.at[:, pl.ds(0, CY), :], face_ref.at[1], sems.at[1]),
        pltpu.make_async_copy(vel_ref, held_ref, sems.at[2]),
    ]
    for copy in copies:
        copy.start()
    messages = []
    for side, which in enumerate((XP, XM)):
        copies[side].wait()
        f = [face_ref[side, i] for i in range(19)]
        fs = relaxed(f, which, *moments(f))
        messages.append([fs[i] for i in which] + [jnp.zeros((CY, NZ), F32)])
    put_messages(inner_ref, outer_ref, *messages)
    copies[2].wait()
    for out in (inner_ref, outer_ref):
        for k in range(3):
            out[5, k : k + 1, 0:PER] = held_ref[k]


def collide_kernel(pop_ref, fs_ref):
    def body(x, carry):
        f = [plane_at(pop_ref, i, x) for i in range(19)]
        fs = relaxed(f, range(19), *moments(f))
        for i in range(19):
            put_plane(fs_ref, i, x, fs[i])
        return carry

    lax.fori_loop(0, CX, body, 0)


def row_kernel(fs_ref, mask_ref, id_ref, inner_ref, outer_ref, own_ref, up_ref, down_ref):
    left_ref, right_ref = neighbours(inner_ref, outer_ref)
    shape = (CX, NZ)
    near, far = tables(left_ref[5], own_ref[5], right_ref[5], shape)
    for y, outward, missing, next_y, out in ((CY - 1, YP, YM, CY - 2, up_ref), (0, YM, YP, 1, down_ref)):
        fs = [x_row(fs_ref, i, y) for i in range(19)]
        masks = [x_row(mask_ref, p, y) for p in range(2)]
        wall = wall_terms(velocity_of(id_ref[pl.ds(y, CX, stride=CY), :], near, far))
        f = [fs[0]]
        for i in range(1, 19):
            cx, cy, cz = DIRS[i]
            back = fs[opp(i)]
            if i in missing:
                moved = jnp.zeros(shape, F32)
            else:
                src_y = next_y if i in outward else y
                moved = x_row(fs_ref, i, src_y) if i in outward else fs[i]
                if cx == 1:
                    moved = x_shifted(moved, 1, left_ref[XP.index(i), src_y : src_y + 1, :], None)
                elif cx == -1:
                    moved = x_shifted(moved, -1, None, right_ref[XM.index(i), src_y : src_y + 1, :])
            if cz != 0:
                if i not in missing:
                    moved = roll(moved, cz, 1)
                moved = jnp.where(z_edge(shape, cz), back, moved)
            f.append(jnp.where(bit_set(masks, opp(i)), back + wall[i], moved))
        rho, mom = moments(f)
        for n, i in enumerate(outward):
            out[n * CX : (n + 1) * CX, :] = fs[i]
            out[(5 + n) * CX : (6 + n) * CX, :] = f[i]
        for n, total in enumerate((rho, *mom)):
            out[(10 + n) * CX : (11 + n) * CX, :] = total
        for p in range(2):
            out[(14 + p) * CX : (15 + p) * CX, :] = masks[p].astype(F32)
        out[256:264, :] = jnp.zeros((8, NZ), F32)
        for i in outward:
            if DIRS[i][0] == 1:
                out[256:257, :] = left_ref[XP.index(i), y : y + 1, :]
            elif DIRS[i][0] == -1:
                out[257:258, :] = right_ref[XM.index(i), y : y + 1, :]


def arrive(fs, source, halo_row, masks, wall):
    shape = (CY, NZ)
    sub = iota(shape, 0)
    f = [fs[0]]
    for i in range(1, 19):
        cx, cy, cz = DIRS[i]
        back = fs[opp(i)]
        moved = source(i)
        if cy != 0:
            moved = roll(moved, cy, 0)
            edge = sub == (0 if cy == 1 else CY - 1)
            moved = jnp.where(edge, halo_row(i), moved)
        if cz != 0:
            moved = jnp.where(z_edge(shape, cz), back, roll(moved, cz, 1))
        f.append(jnp.where(bit_set(masks, opp(i)), back + wall[i], moved))
    return f


HI, LO = 6, 32


def add_hits(masks, values):
    total = [None, None, None]
    for i in range(1, 19):
        term = jnp.where(bit_set(masks, i), values(i), 0.0)
        for k in range(3):
            if DIRS[i][k] != 0:
                if total[k] is None:
                    total[k] = term
                elif DIRS[i][k] == 1:
                    total[k] = total[k] + term
                else:
                    total[k] = total[k] - term
    return [2.0 * t for t in total]


def put_cells(a_ref, b_ref, lanes, ids, force):
    block, member = slots(ids)
    slot = block * PER + member
    hi, lo = jnp.right_shift(slot, 5), jnp.bitwise_and(slot, LO - 1)
    at_hi = [hi == h for h in range(HI)]
    for k in range(3):
        coarse = force[k].astype(jnp.bfloat16).astype(F32)
        for part, value in enumerate((coarse, force[k] - coarse)):
            for h in range(HI):
                row = ((part * 2 + h % 2) * 9 + (h // 2) * 3 + k) * CY
                a_ref[row : row + CY, lanes] = jnp.where(at_hi[h], value, 0.0)
    for v in range(0, LO, 2):
        both = jnp.concatenate([jnp.where(lo == v, 1.0, 0.0), jnp.where(lo == v + 1, 1.0, 0.0)], axis=0)
        b_ref[v * CY : (v + 2) * CY, lanes] = both.astype(jnp.bfloat16)


def sphere_sums(a_ref, b_ref):
    cross = lax.dot_general(
        a_ref[...].astype(jnp.bfloat16), b_ref[...], (((1,), (1,)), ((), ())), preferred_element_type=F32
    )
    cross = cross[: 18 * CY] + cross[18 * CY :]
    same = jnp.bitwise_and(iota(cross.shape, 0), CY - 1) == jnp.bitwise_and(iota(cross.shape, 1), CY - 1)
    cross = jnp.where(same, cross, 0.0)
    column, lane = iota((LO * CY, NZ), 0), iota((LO * CY, NZ), 1)
    sums = None
    for h2 in range(2):
        pick = (jnp.right_shift(column, 3) + h2 * LO == lane).astype(F32)
        part = jnp.dot(
            cross[h2 * 9 * CY : (h2 + 1) * 9 * CY], pick, preferred_element_type=F32, precision=lax.Precision.HIGHEST
        )
        sums = part if sums is None else sums + part
    return [jnp.sum(sums[n * CY : (n + 1) * CY], axis=0, keepdims=True) for n in range(9)]


def first_step_kernel(
    fs_ref, mask_ref, id_ref, inner_ref, outer_ref, own_ref, f_ref, fs2_ref, vel_ref, sum_ref, a_ref, b_ref
):
    left_ref, right_ref = neighbours(inner_ref, outer_ref)
    shape = (CY, NZ)
    near, far = tables(left_ref[5], own_ref[5], right_ref[5], shape)
    sub = iota(shape, 0)
    inside = jnp.logical_and(sub > 0, sub < CY - 1)

    def plane(x, source):
        fs = [plane_at(fs_ref, i, x) for i in range(19)]
        masks = [plane_at(mask_ref, p, x) for p in range(2)]
        start, first = (x * CY, x * NZ) if isinstance(x, int) else (pl.multiple_of(x * CY, CY), pl.multiple_of(x * NZ, NZ))
        ids = id_ref[pl.ds(start, CY), :]
        vel = velocity_of(ids, near, far)
        wall = wall_terms(vel)
        force = add_hits(masks, lambda i: fs[i] - wall[i])
        f = arrive(fs, source, lambda i: 0.0, masks, wall)
        for i in range(19):
            put_plane(f_ref, i, x, f[i])
        fs2 = relaxed(f, range(19), *moments(f))
        for i in range(19):
            put_plane(fs2_ref, i, x, fs2[i])
        more = add_hits(masks, lambda i: fs2[i])
        force = [force[k] + jnp.where(inside, more[k], 0.0) for k in range(3)]
        for k in range(3):
            put_plane(vel_ref, k, x, vel[k])
        put_cells(a_ref, b_ref, pl.ds(first, NZ), ids, force)

    def inner(x, carry):
        plane(x, lambda i: plane_at(fs_ref, i, x - DIRS[i][0]))
        return carry

    plane(0, lambda i: left_ref[XP.index(i)] if i in XP else plane_at(fs_ref, i, 0 - DIRS[i][0]))
    lax.fori_loop(1, CX - 1, inner, 0)
    plane(CX - 1, lambda i: right_ref[XM.index(i)] if i in XM else plane_at(fs_ref, i, CX - 1 - DIRS[i][0]))
    sum_ref[...] = jnp.zeros(sum_ref.shape, F32)
    for n, row in enumerate(sphere_sums(a_ref, b_ref)):
        sum_ref[n : n + 1, :] = row


def second_step_kernel(
    fs_ref, f_ref, fs2_ref, mask_ref, id_ref, sum_ref, inner_ref, outer_ref, below_ref, above_ref,
    row_ref, halo_ref, to_inner_ref, to_outer_ref, mine_ref, a_ref, b_ref,
):
    left_ref, right_ref = neighbours(inner_ref, outer_ref)
    shape = (CX, NZ)
    for side, (y, inward, outward, got) in enumerate(((0, YP, YM, below_ref), (CY - 1, YM, YP, above_ref))):
        masks = [got[(14 + p) * CX : (15 + p) * CX, :].astype(jnp.int32) for p in range(2)]
        rho = got[10 * CX : 11 * CX, :]
        mom = [got[(11 + k) * CX : (12 + k) * CX, :] for k in range(3)]
        for i in outward:
            cx, cy, cz = DIRS[i]
            moved = x_row(fs_ref, i, y)
            if cx == 1:
                moved = x_shifted(moved, 1, left_ref[XP.index(i), y : y + 1, :], None)
            elif cx == -1:
                moved = x_shifted(moved, -1, None, right_ref[XM.index(i), y : y + 1, :])
            held = bit_set(masks, opp(i))
            if cz != 0:
                moved = roll(moved, cz, 1)
                held = jnp.logical_or(held, z_edge(shape, cz))
            moved = jnp.where(held, 0.0, moved)
            rho = rho + moved
            for k in range(3):
                if DIRS[i][k] == 1:
                    mom[k] = mom[k] + moved
                elif DIRS[i][k] == -1:
                    mom[k] = mom[k] - moved
        beyond = relaxed({i: got[(5 + n) * CX : (6 + n) * CX, :] for n, i in enumerate(inward)}, inward, rho, mom)
        for n, i in enumerate(inward):
            halo_ref[side * 5 + n] = beyond[i]

        masks = [x_row(mask_ref, p, y) for p in range(2)]
        f = [x_row(f_ref, i, y) for i in range(19)]
        for n, i in enumerate(inward):
            cx, cy, cz = DIRS[i]
            moved = x_shifted(got[n * CX : (n + 1) * CX, :], cx, got[256:257, :], got[257:258, :])
            held = bit_set(masks, opp(i))
            if cz != 0:
                moved = roll(moved, cz, 1)
                held = jnp.logical_or(held, z_edge(shape, cz))
            f[i] = f[i] + jnp.where(held, 0.0, moved)
        fs = relaxed(f, range(19), *moments(f))
        for i in range(19):
            row_ref[i, side * CX : (side + 1) * CX, :] = fs[i]
        force = add_hits(masks, lambda i: fs[i])
        ids = id_ref[pl.ds(y, CX, stride=CY), :]
        for half in range(2):
            part = slice(half * CY, (half + 1) * CY)
            lanes = slice((side * 2 + half) * NZ, (side * 2 + half + 1) * NZ)
            put_cells(a_ref, b_ref, lanes, ids[part], [t[part] for t in force])

    sub = iota((CY, NZ), 0)
    terms = [row + sum_ref[n : n + 1, :] for n, row in enumerate(sphere_sums(a_ref, b_ref))]
    messages = []
    for which, x, block, corners in ((XP, CX - 1, 2, (7, 9)), (XM, 0, 0, (10, 8))):
        planes = []
        for i in which:
            value = plane_at(fs2_ref, i, x)
            value = jnp.where(sub == 0, row_ref[i, x : x + 1, :], value)
            planes.append(jnp.where(sub == CY - 1, row_ref[i, CX + x : CX + x + 1, :], value))
        rows = [
            halo_ref[YP.index(corners[0]), x : x + 1, :],
            halo_ref[5 + YM.index(corners[1]), x : x + 1, :],
            *terms[block * 3 : block * 3 + 3],
        ]
        packed = jnp.zeros((CY, NZ), F32)
        for n, row in enumerate(rows):
            packed = jnp.where(sub == n, row, packed)
        messages.append(planes + [packed])
    put_messages(to_inner_ref, to_outer_ref, *messages)
    packed = jnp.zeros((CY, NZ), F32)
    for n, row in enumerate(terms[3:6]):
        packed = jnp.where(sub == n + 2, row, packed)
    mine_ref[...] = packed


def halo_slot(i):
    return YP.index(i) if DIRS[i][1] == 1 else 5 + YM.index(i)


def inner_planes_kernel(fs_ref, row_ref, halo_ref, mask_ref, vel_ref, out_ref, edge_ref, all_ref, made_ref, sems):
    for i in range(19):
        all_ref[i] = fs_ref[i]
        all_ref[i, pl.ds(0, CX, stride=CY), :] = row_ref[i, 0:CX, :]
        all_ref[i, pl.ds(CY - 1, CX, stride=CY), :] = row_ref[i, CX : 2 * CX, :]
        edge_ref[i, 0 : 2 * CY, :] = all_ref[i, 0 : 2 * CY, :]
        edge_ref[i, 2 * CY : 4 * CY, :] = all_ref[i, ROWS - 2 * CY : ROWS, :]

    def copy(x):
        rows = pl.ds(pl.multiple_of(x * CY, CY), CY)
        return pltpu.make_async_copy(made_ref.at[:, rows, :], out_ref.at[:, rows, :], sems.at[x])

    def body(x, carry):
        fs = [plane_at(all_ref, i, x) for i in range(19)]
        masks = [plane_at(mask_ref, p, x) for p in range(2)]
        wall = wall_terms([plane_at(vel_ref, k, x) for k in range(3)])
        f = arrive(
            fs,
            lambda i: plane_at(all_ref, i, x - DIRS[i][0]),
            lambda i: halo_ref[halo_slot(i), pl.ds(x - DIRS[i][0], 1), :],
            masks,
            wall,
        )
        for i in range(19):
            put_plane(made_ref, i, x, f[i])
        copy(x).start()
        return carry

    def finish(x, carry):
        copy(x).wait()
        return carry

    lax.fori_loop(1, CX - 1, body, 0)
    lax.fori_loop(1, CX - 1, finish, 0)


def edge_planes_kernel(
    fs_ref, halo_ref, mask_ref, vel_ref, inner_ref, outer_ref, mine_ref, whole_ref, out_ref, force_ref,
    made_ref, total_ref, sems,
):
    del whole_ref
    left_ref, right_ref = neighbours(inner_ref, outer_ref)
    total = mine_ref[...] + left_ref[5] + right_ref[5]
    for k in range(3):
        total_ref[k] = total[2 + k : 3 + k, 0:PER]
    copies = [pltpu.make_async_copy(total_ref, force_ref, sems.at[2])]
    copies[0].start()
    for side, (x, at_x, far_ref, far_dirs) in enumerate(((0, 0, left_ref, XP), (CX - 1, 3, right_ref, XM))):
        fs = [plane_at(fs_ref, i, at_x) for i in range(19)]
        masks = [plane_at(mask_ref, p, x) for p in range(2)]
        wall = wall_terms([plane_at(vel_ref, k, x) for k in range(3)])

        def source(i):
            if i in far_dirs:
                return far_ref[far_dirs.index(i)]
            return plane_at(fs_ref, i, at_x - DIRS[i][0])

        def halo_row(i):
            if i in far_dirs:
                n = 0 if DIRS[i][1] == 1 else 1
                return far_ref[5, n : n + 1, :]
            at = x - DIRS[i][0]
            return halo_ref[halo_slot(i), at : at + 1, :]

        f = arrive(fs, source, halo_row, masks, wall)
        for i in range(19):
            made_ref[side, i] = f[i]
        copy = pltpu.make_async_copy(made_ref.at[side], out_ref.at[:, pl.ds(x * CY, CY), :], sems.at[side])
        copy.start()
        copies.append(copy)
    for copy in copies:
        copy.wait()


def params(limit=VMEM_LIMIT):
    return pltpu.CompilerParams(vmem_limit_bytes=limit)


def cost(flops, nbytes):
    return pl.CostEstimate(flops=flops, bytes_accessed=nbytes, transcendentals=0)


def shape(*dims):
    return jax.ShapeDtypeStruct(dims, F32)


def shift(x, axis, by):
    count = lax.axis_size(axis)
    return lax.ppermute(x, axis, [(i, (i + by) % count) for i in range(count)])


def swap(x, axis, first):
    count = lax.axis_size(axis)
    pairs = [(i % count, (i + 1) % count) for i in range(first, first + count, 2)]
    return lax.ppermute(x, axis, pairs + [(b, a) for a, b in pairs])


def on_device(populations, link_mask, sphere_of_cell, sphere_velocity):
    pops = populations.reshape(19, ROWS, NZ)
    mask = link_mask.reshape(2, ROWS, NZ)
    ids = sphere_of_cell.reshape(ROWS, NZ)
    vel = jnp.transpose(sphere_velocity, (1, 0, 2))
    cells = ROWS * NZ
    xmsg = (6, CY, NZ)
    hbm = pl.BlockSpec(memory_space=pltpu.HBM)
    vmem = pl.BlockSpec(memory_space=pltpu.VMEM)

    to_inner, to_outer = pl.pallas_call(
        face_kernel,
        in_specs=[hbm, hbm],
        out_specs=[vmem, vmem],
        out_shape=[shape(*xmsg)] * 2,
        scratch_shapes=[
            pltpu.VMEM((2, 19, CY, NZ), F32),
            pltpu.VMEM((3, 1, PER), F32),
            pltpu.SemaphoreType.DMA((3,)),
        ],
        compiler_params=params(213 * 256 * 1024),
        name="faces",
    )(pops, vel)
    inner = swap(to_inner, "row", 0)
    outer = swap(to_outer, "row", 1)

    fs1 = pl.pallas_call(
        collide_kernel,
        out_shape=shape(19, ROWS, NZ),
        compiler_params=params(),
        cost_estimate=cost(300 * cells, 38 * 4 * cells),
        name="collide",
    )(pops)

    up, down = pl.pallas_call(
        row_kernel,
        out_shape=[shape(YMSG, NZ)] * 2,
        compiler_params=params(),
        name="y_rows",
    )(fs1, mask, ids, inner, outer, to_inner)
    below = shift(up, "col", 1)
    above = shift(down, "col", -1)

    f1, fs2, cell_vel, sums = pl.pallas_call(
        first_step_kernel,
        out_shape=[shape(19, ROWS, NZ), shape(19, ROWS, NZ), shape(3, ROWS, NZ), shape(16, NZ)],
        scratch_shapes=[
            pltpu.VMEM((2 * 18 * CY, CX * NZ), F32),
            pltpu.VMEM((LO * CY, CX * NZ), jnp.bfloat16),
        ],
        compiler_params=params(),
        cost_estimate=cost(1000 * cells, 70 * 4 * cells),
        name="first_step",
    )(fs1, mask, ids, inner, outer, to_inner)

    rows2, halo, to_inner2, to_outer2, mine = pl.pallas_call(
        second_step_kernel,
        out_shape=[shape(19, 2 * CX, NZ), shape(10, CX, NZ), shape(*xmsg), shape(*xmsg), shape(CY, NZ)],
        scratch_shapes=[
            pltpu.VMEM((2 * 18 * CY, 4 * NZ), F32),
            pltpu.VMEM((LO * CY, 4 * NZ), jnp.bfloat16),
        ],
        compiler_params=params(),
        name="second_step",
    )(fs1, f1, fs2, mask, ids, sums, inner, outer, below, above)
    inner2 = swap(to_inner2, "row", 0)
    outer2 = swap(to_outer2, "row", 1)

    whole, edges = pl.pallas_call(
        inner_planes_kernel,
        out_shape=[shape(19, ROWS, NZ), shape(19, 4 * CY, NZ)],
        out_specs=[hbm, vmem],
        scratch_shapes=[
            pltpu.VMEM((19, ROWS, NZ), F32),
            pltpu.VMEM((19, ROWS, NZ), F32),
            pltpu.SemaphoreType.DMA((CX,)),
        ],
        compiler_params=params(),
        cost_estimate=cost(300 * cells, 45 * 4 * cells),
        name="inner_planes",
    )(fs2, rows2, halo, mask, cell_vel)

    out, force = pl.pallas_call(
        edge_planes_kernel,
        in_specs=[vmem] * 7 + [hbm],
        out_specs=[hbm, hbm],
        out_shape=[shape(19, ROWS, NZ), shape(3, 1, PER)],
        scratch_shapes=[
            pltpu.VMEM((2, 19, CY, NZ), F32),
            pltpu.VMEM((3, 1, PER), F32),
            pltpu.SemaphoreType.DMA((3,)),
        ],
        input_output_aliases={7: 0},
        compiler_params=params(),
        name="edge_planes",
    )(edges, halo, mask, cell_vel, inner2, outer2, mine, whole)

    return out.reshape(19, CX, CY, NZ), jnp.transpose(force, (1, 0, 2))


def solution(mesh):
    in_specs = (
        P(None, "row", "col", None),
        P(None, "row", "col", None),
        P("row", "col", None),
        P("col", None, "row"),
    )
    out_specs = (P(None, "row", "col", None), P("col", None, "row"))
    return jax.shard_map(on_device, mesh=mesh, in_specs=in_specs, out_specs=out_specs, check_vma=False)
```

```python
import jax
import jax.numpy as jnp
from jax import lax
from jax.experimental import pallas as pl
from jax.experimental.pallas import tpu as pltpu
from jax.sharding import PartitionSpec as P

DIRS = (
    (0, 0, 0),
    (1, 0, 0),
    (-1, 0, 0),
    (0, 1, 0),
    (0, -1, 0),
    (0, 0, 1),
    (0, 0, -1),
    (1, 1, 0),
    (-1, -1, 0),
    (1, -1, 0),
    (-1, 1, 0),
    (1, 0, 1),
    (-1, 0, -1),
    (1, 0, -1),
    (-1, 0, 1),
    (0, 1, 1),
    (0, -1, -1),
    (0, 1, -1),
    (0, -1, 1),
)
WEIGHTS = (1.0 / 3.0,) + (1.0 / 18.0,) * 6 + (1.0 / 36.0,) * 12
RELAX = 1.25
F32 = jnp.float32
CX, CY, NZ, PER = 16, 8, 128, 64
ROWS = CX * CY
XP = tuple(i for i in range(19) if DIRS[i][0] == 1)
XM = tuple(i for i in range(19) if DIRS[i][0] == -1)
YP = tuple(i for i in range(19) if DIRS[i][1] == 1)
YM = tuple(i for i in range(19) if DIRS[i][1] == -1)
YMSG = 264
VMEM_LIMIT = 40 * 1024 * 1024


def opp(i):
    return 0 if i == 0 else (i + 1 if i % 2 == 1 else i - 1)


def project(direction, vec):
    total = None
    for k in range(3):
        if direction[k] != 0:
            term = vec[k] if direction[k] == 1 else -vec[k]
            total = term if total is None else total + term
    return total


def bit_set(masks, j):
    return jnp.bitwise_and(masks[(j - 1) // 9], 1 << ((j - 1) % 9)) != 0


def wall_terms(vel):
    terms = [None] * 19
    for i in range(1, 19, 2):
        along = (6.0 * WEIGHTS[i]) * project(DIRS[i], vel)
        terms[i] = along
        terms[i + 1] = -along
    return terms


def moments(f):
    rho = f[0]
    for i in range(1, 19):
        rho = rho + f[i]
    mom = []
    for k in range(3):
        total = None
        for i in range(19):
            if DIRS[i][k] != 0:
                if total is None:
                    total = f[i]
                elif DIRS[i][k] == 1:
                    total = total + f[i]
                else:
                    total = total - f[i]
        mom.append(total)
    return rho, mom


def relaxed(f, which, rho, mom):
    inv = 1.0 / rho
    u = [m * inv for m in mom]
    base = 1.0 - 1.5 * (u[0] * u[0] + u[1] * u[1] + u[2] * u[2])
    out = {}
    scaled = {w: (RELAX * w) * rho for w in sorted({WEIGHTS[i] for i in which})}
    for i in which:
        if i == 0:
            shape = base
        else:
            along = project(DIRS[i], u)
            shape = base + along * (3.0 + 4.5 * along)
        out[i] = (1.0 - RELAX) * f[i] + scaled[WEIGHTS[i]] * shape
    return out


def iota(shape, dim):
    return lax.broadcasted_iota(jnp.int32, shape, dim)


def roll(x, by, axis):
    return pltpu.roll(x, by % x.shape[axis], axis)


def slots(ids):
    count = lax.axis_size("row")
    block = jnp.right_shift(ids, 6) - lax.axis_index("row") + 1
    block = jnp.where(block < 0, block + count, block)
    block = jnp.where(block >= count, block - count, block)
    return block, jnp.bitwise_and(ids, PER - 1)


def tables(left, own, right, shape):
    low = iota((8, NZ), 1) < PER
    pair = jnp.where(low, left, roll(own, PER, 1))
    near = [jnp.broadcast_to(pair[k : k + 1], shape) for k in range(3)]
    far = [jnp.broadcast_to(right[k : k + 1], shape) for k in range(3)]
    return near, far


def velocity_of(ids, near, far):
    block, member = slots(ids)
    index = jnp.where(block == 1, member + PER, member)
    is_far = block == 2
    out = []
    for k in range(3):
        a = jnp.take_along_axis(near[k], index, axis=1, mode="promise_in_bounds")
        b = jnp.take_along_axis(far[k], index, axis=1, mode="promise_in_bounds")
        out.append(jnp.where(is_far, b, a))
    return out


def z_edge(shape, step):
    return iota(shape, 1) == (0 if step == 1 else NZ - 1)


def plane_at(ref, i, x):
    start = x * CY if isinstance(x, int) else pl.multiple_of(x * CY, CY)
    return ref[i, pl.ds(start, CY), :]


def put_plane(ref, i, x, value):
    start = x * CY if isinstance(x, int) else pl.multiple_of(x * CY, CY)
    ref[i, pl.ds(start, CY), :] = value


def x_row(ref, i, y):
    return ref[i, pl.ds(y, CX, stride=CY), :]


def x_shifted(row, step, left, right):
    if step == 0:
        return row
    at = iota((CX, NZ), 0)
    if step == 1:
        return jnp.where(at == 0, left, roll(row, 1, 0))
    return jnp.where(at == CX - 1, right, roll(row, -1, 0))


def even_row():
    return lax.rem(lax.axis_index("row"), 2) == 0


class Either:
    def __init__(self, even, if_even, if_odd):
        self.even, self.if_even, self.if_odd = even, if_even, if_odd

    def __getitem__(self, at):
        return jnp.where(self.even, self.if_even[at], self.if_odd[at])


def neighbours(inner_ref, outer_ref):
    even = even_row()
    return Either(even, outer_ref, inner_ref), Either(even, inner_ref, outer_ref)


def put_messages(inner_ref, outer_ref, to_right, to_left):
    even = even_row()
    for n in range(6):
        inner_ref[n] = jnp.where(even, to_right[n], to_left[n])
        outer_ref[n] = jnp.where(even, to_left[n], to_right[n])


def face_kernel(pop_ref, vel_ref, inner_ref, outer_ref, face_ref, held_ref, sems):
    copies = [
        pltpu.make_async_copy(pop_ref.at[:, pl.ds(ROWS - CY, CY), :], face_ref.at[0], sems.at[0]),
        pltpu.make_async_copy(pop_ref.at[:, pl.ds(0, CY), :], face_ref.at[1], sems.at[1]),
        pltpu.make_async_copy(vel_ref, held_ref, sems.at[2]),
    ]
    for copy in copies:
        copy.start()
    messages = []
    for side, which in enumerate((XP, XM)):
        copies[side].wait()
        f = [face_ref[side, i] for i in range(19)]
        fs = relaxed(f, which, *moments(f))
        messages.append([fs[i] for i in which] + [jnp.zeros((CY, NZ), F32)])
    put_messages(inner_ref, outer_ref, *messages)
    copies[2].wait()
    for out in (inner_ref, outer_ref):
        for k in range(3):
            out[5, k : k + 1, 0:PER] = held_ref[k]


def collide_kernel(pop_ref, fs_ref):
    def body(x, carry):
        f = [plane_at(pop_ref, i, x) for i in range(19)]
        fs = relaxed(f, range(19), *moments(f))
        for i in range(19):
            put_plane(fs_ref, i, x, fs[i])
        return carry

    lax.fori_loop(0, CX, body, 0)


def row_kernel(fs_ref, mask_ref, id_ref, inner_ref, outer_ref, own_ref, up_ref, down_ref):
    left_ref, right_ref = neighbours(inner_ref, outer_ref)
    shape = (CX, NZ)
    near, far = tables(left_ref[5], own_ref[5], right_ref[5], shape)
    for y, outward, missing, next_y, out in ((CY - 1, YP, YM, CY - 2, up_ref), (0, YM, YP, 1, down_ref)):
        fs = [x_row(fs_ref, i, y) for i in range(19)]
        masks = [x_row(mask_ref, p, y) for p in range(2)]
        wall = wall_terms(velocity_of(id_ref[pl.ds(y, CX, stride=CY), :], near, far))
        f = [fs[0]]
        for i in range(1, 19):
            cx, cy, cz = DIRS[i]
            back = fs[opp(i)]
            if i in missing:
                moved = jnp.zeros(shape, F32)
            else:
                src_y = next_y if i in outward else y
                moved = x_row(fs_ref, i, src_y) if i in outward else fs[i]
                if cx == 1:
                    moved = x_shifted(moved, 1, left_ref[XP.index(i), src_y : src_y + 1, :], None)
                elif cx == -1:
                    moved = x_shifted(moved, -1, None, right_ref[XM.index(i), src_y : src_y + 1, :])
            if cz != 0:
                if i not in missing:
                    moved = roll(moved, cz, 1)
                moved = jnp.where(z_edge(shape, cz), back, moved)
            f.append(jnp.where(bit_set(masks, opp(i)), back + wall[i], moved))
        rho, mom = moments(f)
        for n, i in enumerate(outward):
            out[n * CX : (n + 1) * CX, :] = fs[i]
            out[(5 + n) * CX : (6 + n) * CX, :] = f[i]
        for n, total in enumerate((rho, *mom)):
            out[(10 + n) * CX : (11 + n) * CX, :] = total
        for p in range(2):
            out[(14 + p) * CX : (15 + p) * CX, :] = masks[p].astype(F32)
        out[256:264, :] = jnp.zeros((8, NZ), F32)
        for i in outward:
            if DIRS[i][0] == 1:
                out[256:257, :] = left_ref[XP.index(i), y : y + 1, :]
            elif DIRS[i][0] == -1:
                out[257:258, :] = right_ref[XM.index(i), y : y + 1, :]


def arrive(fs, source, halo_row, masks, wall):
    shape = (CY, NZ)
    sub = iota(shape, 0)
    f = [fs[0]]
    for i in range(1, 19):
        cx, cy, cz = DIRS[i]
        back = fs[opp(i)]
        moved = source(i)
        if cy != 0:
            moved = roll(moved, cy, 0)
            edge = sub == (0 if cy == 1 else CY - 1)
            moved = jnp.where(edge, halo_row(i), moved)
        if cz != 0:
            moved = jnp.where(z_edge(shape, cz), back, roll(moved, cz, 1))
        f.append(jnp.where(bit_set(masks, opp(i)), back + wall[i], moved))
    return f


HI, LO = 6, 32


def add_hits(masks, values):
    total = [None, None, None]
    for i in range(1, 19):
        term = jnp.where(bit_set(masks, i), values(i), 0.0)
        for k in range(3):
            if DIRS[i][k] != 0:
                if total[k] is None:
                    total[k] = term
                elif DIRS[i][k] == 1:
                    total[k] = total[k] + term
                else:
                    total[k] = total[k] - term
    return [2.0 * t for t in total]


def put_cells(a_ref, b_ref, lanes, ids, force):
    block, member = slots(ids)
    slot = block * PER + member
    hi, lo = jnp.right_shift(slot, 5), jnp.bitwise_and(slot, LO - 1)
    at_hi = [hi == h for h in range(HI)]
    for k in range(3):
        coarse = force[k].astype(jnp.bfloat16).astype(F32)
        for part, value in enumerate((coarse, force[k] - coarse)):
            for h in range(HI):
                row = ((part * 2 + h % 2) * 9 + (h // 2) * 3 + k) * CY
                a_ref[row : row + CY, lanes] = jnp.where(at_hi[h], value, 0.0)
    for v in range(0, LO, 2):
        both = jnp.concatenate([jnp.where(lo == v, 1.0, 0.0), jnp.where(lo == v + 1, 1.0, 0.0)], axis=0)
        b_ref[v * CY : (v + 2) * CY, lanes] = both.astype(jnp.bfloat16)


def sphere_sums(a_ref, b_ref):
    cross = lax.dot_general(
        a_ref[...].astype(jnp.bfloat16), b_ref[...], (((1,), (1,)), ((), ())), preferred_element_type=F32
    )
    cross = cross[: 18 * CY] + cross[18 * CY :]
    same = jnp.bitwise_and(iota(cross.shape, 0), CY - 1) == jnp.bitwise_and(iota(cross.shape, 1), CY - 1)
    cross = jnp.where(same, cross, 0.0)
    column, lane = iota((LO * CY, NZ), 0), iota((LO * CY, NZ), 1)
    sums = None
    for h2 in range(2):
        pick = (jnp.right_shift(column, 3) + h2 * LO == lane).astype(F32)
        part = jnp.dot(
            cross[h2 * 9 * CY : (h2 + 1) * 9 * CY], pick, preferred_element_type=F32, precision=lax.Precision.HIGHEST
        )
        sums = part if sums is None else sums + part
    return [jnp.sum(sums[n * CY : (n + 1) * CY], axis=0, keepdims=True) for n in range(9)]


def first_step_kernel(
    fs_ref, mask_ref, id_ref, inner_ref, outer_ref, own_ref, f_ref, fs2_ref, vel_ref, sum_ref, a_ref, b_ref
):
    left_ref, right_ref = neighbours(inner_ref, outer_ref)
    shape = (CY, NZ)
    near, far = tables(left_ref[5], own_ref[5], right_ref[5], shape)
    sub = iota(shape, 0)
    inside = jnp.logical_and(sub > 0, sub < CY - 1)

    def plane(x, source):
        fs = [plane_at(fs_ref, i, x) for i in range(19)]
        masks = [plane_at(mask_ref, p, x) for p in range(2)]
        start, first = (x * CY, x * NZ) if isinstance(x, int) else (pl.multiple_of(x * CY, CY), pl.multiple_of(x * NZ, NZ))
        ids = id_ref[pl.ds(start, CY), :]
        vel = velocity_of(ids, near, far)
        wall = wall_terms(vel)
        force = add_hits(masks, lambda i: fs[i] - wall[i])
        f = arrive(fs, source, lambda i: 0.0, masks, wall)
        for i in range(19):
            put_plane(f_ref, i, x, f[i])
        fs2 = relaxed(f, range(19), *moments(f))
        for i in range(19):
            put_plane(fs2_ref, i, x, fs2[i])
        more = add_hits(masks, lambda i: fs2[i])
        force = [force[k] + jnp.where(inside, more[k], 0.0) for k in range(3)]
        for k in range(3):
            put_plane(vel_ref, k, x, vel[k])
        put_cells(a_ref, b_ref, pl.ds(first, NZ), ids, force)

    def inner(x, carry):
        plane(x, lambda i: plane_at(fs_ref, i, x - DIRS[i][0]))
        return carry

    plane(0, lambda i: left_ref[XP.index(i)] if i in XP else plane_at(fs_ref, i, 0 - DIRS[i][0]))
    lax.fori_loop(1, CX - 1, inner, 0)
    plane(CX - 1, lambda i: right_ref[XM.index(i)] if i in XM else plane_at(fs_ref, i, CX - 1 - DIRS[i][0]))
    sum_ref[...] = jnp.zeros(sum_ref.shape, F32)
    for n, row in enumerate(sphere_sums(a_ref, b_ref)):
        sum_ref[n : n + 1, :] = row


def second_step_kernel(
    fs_ref, f_ref, fs2_ref, mask_ref, id_ref, sum_ref, inner_ref, outer_ref, below_ref, above_ref,
    row_ref, halo_ref, to_inner_ref, to_outer_ref, mine_ref, a_ref, b_ref,
):
    left_ref, right_ref = neighbours(inner_ref, outer_ref)
    shape = (CX, NZ)
    for side, (y, inward, outward, got) in enumerate(((0, YP, YM, below_ref), (CY - 1, YM, YP, above_ref))):
        masks = [got[(14 + p) * CX : (15 + p) * CX, :].astype(jnp.int32) for p in range(2)]
        rho = got[10 * CX : 11 * CX, :]
        mom = [got[(11 + k) * CX : (12 + k) * CX, :] for k in range(3)]
        for i in outward:
            cx, cy, cz = DIRS[i]
            moved = x_row(fs_ref, i, y)
            if cx == 1:
                moved = x_shifted(moved, 1, left_ref[XP.index(i), y : y + 1, :], None)
            elif cx == -1:
                moved = x_shifted(moved, -1, None, right_ref[XM.index(i), y : y + 1, :])
            held = bit_set(masks, opp(i))
            if cz != 0:
                moved = roll(moved, cz, 1)
                held = jnp.logical_or(held, z_edge(shape, cz))
            moved = jnp.where(held, 0.0, moved)
            rho = rho + moved
            for k in range(3):
                if DIRS[i][k] == 1:
                    mom[k] = mom[k] + moved
                elif DIRS[i][k] == -1:
                    mom[k] = mom[k] - moved
        beyond = relaxed({i: got[(5 + n) * CX : (6 + n) * CX, :] for n, i in enumerate(inward)}, inward, rho, mom)
        for n, i in enumerate(inward):
            halo_ref[side * 5 + n] = beyond[i]

        masks = [x_row(mask_ref, p, y) for p in range(2)]
        f = [x_row(f_ref, i, y) for i in range(19)]
        for n, i in enumerate(inward):
            cx, cy, cz = DIRS[i]
            moved = x_shifted(got[n * CX : (n + 1) * CX, :], cx, got[256:257, :], got[257:258, :])
            held = bit_set(masks, opp(i))
            if cz != 0:
                moved = roll(moved, cz, 1)
                held = jnp.logical_or(held, z_edge(shape, cz))
            f[i] = f[i] + jnp.where(held, 0.0, moved)
        fs = relaxed(f, range(19), *moments(f))
        for i in range(19):
            row_ref[i, side * CX : (side + 1) * CX, :] = fs[i]
        force = add_hits(masks, lambda i: fs[i])
        ids = id_ref[pl.ds(y, CX, stride=CY), :]
        for half in range(2):
            part = slice(half * CY, (half + 1) * CY)
            lanes = slice((side * 2 + half) * NZ, (side * 2 + half + 1) * NZ)
            put_cells(a_ref, b_ref, lanes, ids[part], [t[part] for t in force])

    sub = iota((CY, NZ), 0)
    terms = [row + sum_ref[n : n + 1, :] for n, row in enumerate(sphere_sums(a_ref, b_ref))]
    messages = []
    for which, x, block, corners in ((XP, CX - 1, 2, (7, 9)), (XM, 0, 0, (10, 8))):
        planes = []
        for i in which:
            value = plane_at(fs2_ref, i, x)
            value = jnp.where(sub == 0, row_ref[i, x : x + 1, :], value)
            planes.append(jnp.where(sub == CY - 1, row_ref[i, CX + x : CX + x + 1, :], value))
        rows = [
            halo_ref[YP.index(corners[0]), x : x + 1, :],
            halo_ref[5 + YM.index(corners[1]), x : x + 1, :],
            *terms[block * 3 : block * 3 + 3],
        ]
        packed = jnp.zeros((CY, NZ), F32)
        for n, row in enumerate(rows):
            packed = jnp.where(sub == n, row, packed)
        messages.append(planes + [packed])
    put_messages(to_inner_ref, to_outer_ref, *messages)
    packed = jnp.zeros((CY, NZ), F32)
    for n, row in enumerate(terms[3:6]):
        packed = jnp.where(sub == n + 2, row, packed)
    mine_ref[...] = packed


def halo_slot(i):
    return YP.index(i) if DIRS[i][1] == 1 else 5 + YM.index(i)


def inner_planes_kernel(fs_ref, row_ref, halo_ref, mask_ref, vel_ref, out_ref, edge_ref, all_ref, made_ref, sems):
    for i in range(19):
        all_ref[i] = fs_ref[i]
        all_ref[i, pl.ds(0, CX, stride=CY), :] = row_ref[i, 0:CX, :]
        all_ref[i, pl.ds(CY - 1, CX, stride=CY), :] = row_ref[i, CX : 2 * CX, :]
        edge_ref[i, 0 : 2 * CY, :] = all_ref[i, 0 : 2 * CY, :]
        edge_ref[i, 2 * CY : 4 * CY, :] = all_ref[i, ROWS - 2 * CY : ROWS, :]

    def copy(x):
        rows = pl.ds(pl.multiple_of(x * CY, CY), CY)
        return pltpu.make_async_copy(made_ref.at[:, rows, :], out_ref.at[:, rows, :], sems.at[x])

    def body(x, carry):
        fs = [plane_at(all_ref, i, x) for i in range(19)]
        masks = [plane_at(mask_ref, p, x) for p in range(2)]
        wall = wall_terms([plane_at(vel_ref, k, x) for k in range(3)])
        f = arrive(
            fs,
            lambda i: plane_at(all_ref, i, x - DIRS[i][0]),
            lambda i: halo_ref[halo_slot(i), pl.ds(x - DIRS[i][0], 1), :],
            masks,
            wall,
        )
        for i in range(19):
            put_plane(made_ref, i, x, f[i])
        copy(x).start()
        return carry

    def finish(x, carry):
        copy(x).wait()
        return carry

    lax.fori_loop(1, CX - 1, body, 0)
    lax.fori_loop(1, CX - 1, finish, 0)


def edge_planes_kernel(
    fs_ref, halo_ref, mask_ref, vel_ref, outer_ref, inner_ref, mine_ref, whole_ref, out_ref, force_ref,
    made_ref, total_ref, sems,
):
    del whole_ref
    left_ref, right_ref = neighbours(inner_ref, outer_ref)
    total = mine_ref[...] + left_ref[5] + right_ref[5]
    for k in range(3):
        total_ref[k] = total[2 + k : 3 + k, 0:PER]
    copies = [pltpu.make_async_copy(total_ref, force_ref, sems.at[2])]
    copies[0].start()
    for side, (x, at_x, far_ref, far_dirs) in enumerate(((0, 0, left_ref, XP), (CX - 1, 3, right_ref, XM))):
        fs = [plane_at(fs_ref, i, at_x) for i in range(19)]
        masks = [plane_at(mask_ref, p, x) for p in range(2)]
        wall = wall_terms([plane_at(vel_ref, k, x) for k in range(3)])

        def source(i):
            if i in far_dirs:
                return far_ref[far_dirs.index(i)]
            return plane_at(fs_ref, i, at_x - DIRS[i][0])

        def halo_row(i):
            if i in far_dirs:
                n = 0 if DIRS[i][1] == 1 else 1
                return far_ref[5, n : n + 1, :]
            at = x - DIRS[i][0]
            return halo_ref[halo_slot(i), at : at + 1, :]

        f = arrive(fs, source, halo_row, masks, wall)
        for i in range(19):
            made_ref[side, i] = f[i]
        copy = pltpu.make_async_copy(made_ref.at[side], out_ref.at[:, pl.ds(x * CY, CY), :], sems.at[side])
        copy.start()
        copies.append(copy)
    for copy in copies:
        copy.wait()


def params(limit=VMEM_LIMIT):
    return pltpu.CompilerParams(vmem_limit_bytes=limit)


def cost(flops, nbytes):
    return pl.CostEstimate(flops=flops, bytes_accessed=nbytes, transcendentals=0)


def shape(*dims):
    return jax.ShapeDtypeStruct(dims, F32)


def shift(x, axis, by):
    count = lax.axis_size(axis)
    return lax.ppermute(x, axis, [(i, (i + by) % count) for i in range(count)])


def swap(x, axis, first):
    count = lax.axis_size(axis)
    pairs = [(i % count, (i + 1) % count) for i in range(first, first + count, 2)]
    return lax.ppermute(x, axis, pairs + [(b, a) for a, b in pairs])


def on_device(populations, link_mask, sphere_of_cell, sphere_velocity):
    pops = populations.reshape(19, ROWS, NZ)
    mask = link_mask.reshape(2, ROWS, NZ)
    ids = sphere_of_cell.reshape(ROWS, NZ)
    vel = jnp.transpose(sphere_velocity, (1, 0, 2))
    vel = pltpu.with_memory_space_constraint(vel, pltpu.HBM)
    cells = ROWS * NZ
    xmsg = (6, CY, NZ)
    hbm = pl.BlockSpec(memory_space=pltpu.HBM)
    vmem = pl.BlockSpec(memory_space=pltpu.VMEM)

    to_inner, to_outer = pl.pallas_call(
        face_kernel,
        in_specs=[hbm, hbm],
        out_specs=[vmem, vmem],
        out_shape=[shape(*xmsg)] * 2,
        scratch_shapes=[
            pltpu.VMEM((2, 19, CY, NZ), F32),
            pltpu.VMEM((3, 1, PER), F32),
            pltpu.SemaphoreType.DMA((3,)),
        ],
        compiler_params=params(213 * 256 * 1024),
        name="faces",
    )(pops, vel)
    inner = swap(to_inner, "row", 0)
    outer = swap(to_outer, "row", 1)

    fs1 = pl.pallas_call(
        collide_kernel,
        out_shape=shape(19, ROWS, NZ),
        compiler_params=params(),
        cost_estimate=cost(300 * cells, 38 * 4 * cells),
        name="collide",
    )(pops)

    up, down = pl.pallas_call(
        row_kernel,
        out_shape=[shape(YMSG, NZ)] * 2,
        compiler_params=params(),
        name="y_rows",
    )(fs1, mask, ids, inner, outer, to_inner)
    below = shift(up, "col", 1)
    above = shift(down, "col", -1)

    f1, fs2, cell_vel, sums = pl.pallas_call(
        first_step_kernel,
        out_shape=[shape(19, ROWS, NZ), shape(19, ROWS, NZ), shape(3, ROWS, NZ), shape(16, NZ)],
        scratch_shapes=[
            pltpu.VMEM((2 * 18 * CY, CX * NZ), F32),
            pltpu.VMEM((LO * CY, CX * NZ), jnp.bfloat16),
        ],
        compiler_params=params(),
        cost_estimate=cost(1000 * cells, 70 * 4 * cells),
        name="first_step",
    )(fs1, mask, ids, inner, outer, to_inner)

    rows2, halo, to_inner2, to_outer2, mine = pl.pallas_call(
        second_step_kernel,
        out_shape=[shape(19, 2 * CX, NZ), shape(10, CX, NZ), shape(*xmsg), shape(*xmsg), shape(CY, NZ)],
        scratch_shapes=[
            pltpu.VMEM((2 * 18 * CY, 4 * NZ), F32),
            pltpu.VMEM((LO * CY, 4 * NZ), jnp.bfloat16),
        ],
        compiler_params=params(),
        name="second_step",
    )(fs1, f1, fs2, mask, ids, sums, inner, outer, below, above)
    inner2 = swap(to_inner2, "row", 0)
    outer2 = swap(to_outer2, "row", 1)

    whole, edges = pl.pallas_call(
        inner_planes_kernel,
        out_shape=[shape(19, ROWS, NZ), shape(19, 4 * CY, NZ)],
        out_specs=[hbm, vmem],
        scratch_shapes=[
            pltpu.VMEM((19, ROWS, NZ), F32),
            pltpu.VMEM((19, ROWS, NZ), F32),
            pltpu.SemaphoreType.DMA((CX,)),
        ],
        compiler_params=params(),
        cost_estimate=cost(300 * cells, 45 * 4 * cells),
        name="inner_planes",
    )(fs2, rows2, halo, mask, cell_vel)

    out, force = pl.pallas_call(
        edge_planes_kernel,
        in_specs=[vmem] * 7 + [hbm],
        out_specs=[hbm, hbm],
        out_shape=[shape(19, ROWS, NZ), shape(3, 1, PER)],
        scratch_shapes=[
            pltpu.VMEM((2, 19, CY, NZ), F32),
            pltpu.VMEM((3, 1, PER), F32),
            pltpu.SemaphoreType.DMA((3,)),
        ],
        input_output_aliases={7: 0},
        compiler_params=params(),
        name="edge_planes",
    )(edges, halo, mask, cell_vel, outer2, inner2, mine, whole)

    return out.reshape(19, CX, CY, NZ), jnp.transpose(force, (1, 0, 2))


def solution(mesh):
    in_specs = (
        P(None, "row", "col", None),
        P(None, "row", "col", None),
        P("row", "col", None),
        P("col", None, "row"),
    )
    out_specs = (P(None, "row", "col", None), P("col", None, "row"))
    return jax.shard_map(on_device, mesh=mesh, in_specs=in_specs, out_specs=out_specs, check_vma=False)
```
